32 devices in a mesh: groups: 2 (over y), ctx: 16 (over z, x, core).
Axes of the slice: x: 2, y: 2, z: 4, core: 2. Of those that a mesh axis runs over, the one named last changes fastest.
Arguments:
- queries: bfloat16 [4096, 2560], P(('groups', 'ctx')), parts along dimension 0, may hold values from -6 to 6
- key_states: bfloat16 [4096, 2560], P(('groups', 'ctx')), parts along dimension 0, may hold values from -6 to 6
- value_states: bfloat16 [4096, 2560], P(('groups', 'ctx')), parts along dimension 0, may hold values from -6 to 6
- out_grads: bfloat16 [4096, 2560], P(('groups', 'ctx')), parts along dimension 0, may hold values from -6 to 6
- log_norms: bfloat16 [20, 4096], P(None, ('groups', 'ctx')), parts along dimension 1, may hold values from 6.5 to 8.5
- row_deltas: bfloat16 [20, 4096], P(None, ('groups', 'ctx')), parts along dimension 1, may hold values from -24 to 24
- kv_blocks: int32 [16, 7], replicated, may hold values from -1 to 15, as said below
Outputs:
- query_grads: bfloat16 [4096, 2560], P(('groups', 'ctx')), parts along dimension 0
- key_grads: bfloat16 [4096, 2560], P(('groups', 'ctx')), parts along dimension 0
- value_grads: bfloat16 [4096, 2560], P(('groups', 'ctx')), parts along dimension 0
The draws below stay inside these ranges and needn't reach their ends.
There are 2 independent parts, one for each index of `groups`. The reference program is written for one: setup_inputs(seed, part) draws one part's arguments, and reference() takes and returns one part's arrays. A program takes and returns all parts, laid end to end along the dimension named above; an argument that names none is the same for every part. Nothing has to cross between parts.
Inputs may be any that keep to these rules, and one draw needn't show every extreme that they name: `kv_blocks`: row b lists distinct blocks in any order of its slots, the rest -1: the blocks b - 1, b and b + 1 that lie in 0 to 15, and otherwise only blocks whose group index k // 1 differs from b // 1 by + or - 2 ** j with 1 <= j <= 2. For each group of 1 query block and each such other group, at most one entry in all of the group's rows names a block of the other group.
All inputs are finite; a program needn't handle non-finite values.
Results may differ from the reference program's by a relative error of at most 0.0049.
Values may be sent and summed in bfloat16 or wider, within the bound.
A program may use at most 128 MiB of HBM per device.

```python
import jax
import jax.numpy as jnp
from jax import lax

HEADS = 20
HEAD_DIM = 128
BLK = 128
LEVELS = 2
BPD = 1
TOKENS = 2048
NB = 16
KMAX = 7


def draw_kv_blocks(key, part):
    key = jax.random.fold_in(key, 11)
    groups_count = NB // BPD
    block_idx = jnp.arange(NB, dtype=jnp.int32)
    owner_dev = block_idx // BPD
    local_idx = block_idx % BPD
    before_blk = jnp.where(block_idx >= 1, block_idx - 1, -1)
    after_blk = jnp.where(block_idx + 1 < NB, block_idx + 1, -1)
    columns = [before_blk, block_idx, after_blk]
    counter = 0
    for rung_idx in range(1, LEVELS + 1):
        for direction in (1, -1):
            counter = counter + 1
            level_key = jax.random.fold_in(key, counter)
            pick_key, query_key, block_key = jax.random.split(level_key, 3)
            chosen = jax.random.randint(pick_key, (groups_count,), 0, 4) < 3
            query_pick = jax.random.randint(query_key, (groups_count,), 0, BPD)
            key_pick = jax.random.randint(block_key, (groups_count,), 0, BPD)
            partner = jnp.arange(groups_count, dtype=jnp.int32) + direction * 2 ** rung_idx
            usable = chosen & (partner >= 0) & (partner < groups_count)
            target = partner * BPD + key_pick
            column = jnp.where(usable[owner_dev] & (query_pick[owner_dev] == local_idx), target[owner_dev], -1)
            columns.append(column)
    listing = jnp.stack(columns, axis=1)
    order_key = jax.random.fold_in(key, 97)
    rank_keys = jax.random.randint(order_key, (NB, KMAX), 0, 1024) * KMAX + jnp.arange(KMAX, dtype=jnp.int32)[None, :]
    shuffle = jnp.argsort(rank_keys, axis=1)
    return jnp.take_along_axis(listing, shuffle, axis=1).astype(jnp.int32)


def block_scale(key, extent, cuts, smallest, largest):
    def one(dim, parts):
        heights = jax.random.uniform(jax.random.fold_in(jax.random.fold_in(key, 6), dim), (parts,), jnp.float32, smallest / len(cuts), largest / len(cuts))
        return jnp.repeat(jnp.exp(heights), extent[dim] // parts).reshape((-1,) + (1,) * (len(extent) - dim - 1))

    gain = one(*cuts[0])
    for cut in cuts[1:]:
        gain = gain * one(*cut)
    return gain


def bell_draw(own_key, shape, deviation, limit, pieces=(), kind=jnp.bfloat16):
    drawn = jax.random.normal(own_key, shape, jnp.float32) * deviation
    if len(pieces) > 0:
        drawn = block_scale(own_key, shape, pieces, -0.22, 0.18) * drawn
    return jnp.clip(drawn, min=-limit, max=limit).astype(kind)


def setup_inputs(seed: int = 0, part: int = 0) -> dict:
    splits = jax.random.split(jax.random.key(seed), 8)
    part_splits = jax.random.split(jax.random.fold_in(splits[7], part), 8)
    queries = bell_draw(part_splits[0], (TOKENS, HEADS * HEAD_DIM), 1.0, 6.0, ((0, 16),))
    key_states = bell_draw(part_splits[1], (TOKENS, HEADS * HEAD_DIM), 1.0, 6.0, ((0, 16),))
    value_states = bell_draw(part_splits[2], (TOKENS, HEADS * HEAD_DIM), 1.0, 6.0, ((0, 16),))
    out_grads = bell_draw(part_splits[3], (TOKENS, HEADS * HEAD_DIM), 1.0, 6.0, ((0, 16),))
    log_norms = jnp.clip(6.5 + 2.0 * jax.random.uniform(part_splits[4], (HEADS, TOKENS), jnp.float32) ** block_scale(part_splits[4], (HEADS, TOKENS), ((1, 16),), -0.2, 0.2), 6.5, 8.5).astype(jnp.bfloat16)
    row_deltas = bell_draw(part_splits[5], (HEADS, TOKENS), 4.0, 24.0, ((1, 16),))
    kv_blocks = draw_kv_blocks(jax.random.fold_in(splits[7], 71), part)
    return {"queries": queries, "key_states": key_states, "value_states": value_states, "out_grads": out_grads, "log_norms": log_norms, "row_deltas": row_deltas, "kv_blocks": kv_blocks}


def grads_tile(query_tile, grad_tile, norm_tile, delta_tile, key_tile, value_tile, weights):
    head_dim = query_tile.shape[-1]
    factor = head_dim ** -0.5
    scores = jnp.einsum("qhd,khd->hqk", query_tile.astype(jnp.float32), key_tile.astype(jnp.float32)) * factor
    probs = jnp.exp(scores - norm_tile.astype(jnp.float32)[:, :, None]) * weights[None, None, :]
    probs_low = probs.astype(jnp.bfloat16)
    dprobs = jnp.einsum("qhd,khd->hqk", grad_tile.astype(jnp.float32), value_tile.astype(jnp.float32))
    dscores = (probs * (dprobs - delta_tile.astype(jnp.float32)[:, :, None])).astype(jnp.bfloat16)
    value_part = jnp.einsum("hqk,qhd->khd", probs_low.astype(jnp.float32), grad_tile.astype(jnp.float32))
    key_part = jnp.einsum("hqk,qhd->khd", dscores.astype(jnp.float32), query_tile.astype(jnp.float32)) * factor
    query_part = jnp.einsum("hqk,khd->qhd", dscores.astype(jnp.float32), key_tile.astype(jnp.float32)) * factor
    return query_part, key_part, value_part


def reference(queries, key_states, value_states, out_grads, log_norms, row_deltas, kv_blocks):
    width = queries.shape[1]
    head_dim = width // HEADS
    query_blk = queries.reshape(NB, BLK, HEADS, head_dim)
    grad_blk = out_grads.reshape(NB, BLK, HEADS, head_dim)
    key_blk = key_states.reshape(NB, BLK, HEADS, head_dim)
    value_blk = value_states.reshape(NB, BLK, HEADS, head_dim)
    norm_blk = log_norms.reshape(HEADS, NB, BLK).transpose(1, 0, 2)
    delta_blk = row_deltas.reshape(HEADS, NB, BLK).transpose(1, 0, 2)
    initial = (jnp.zeros((NB, BLK, HEADS, head_dim), jnp.float32), jnp.zeros((NB, BLK, HEADS, head_dim), jnp.float32))

    def visit_block(carry, block_idx):
        key_acc, value_acc = carry
        listed = kv_blocks[block_idx]
        inside = listed >= 0
        safe_idx = jnp.where(inside, listed, 0).astype(jnp.int32)
        gathered_keys = key_blk[safe_idx].reshape(KMAX * BLK, HEADS, head_dim)
        gathered_values = value_blk[safe_idx].reshape(KMAX * BLK, HEADS, head_dim)
        weights = jnp.repeat(inside.astype(jnp.float32), BLK)
        query_part, key_part, value_part = grads_tile(query_blk[block_idx], grad_blk[block_idx], norm_blk[block_idx], delta_blk[block_idx], gathered_keys, gathered_values, weights)
        key_acc = key_acc.at[safe_idx].add(key_part.reshape(KMAX, BLK, HEADS, head_dim))
        value_acc = value_acc.at[safe_idx].add(value_part.reshape(KMAX, BLK, HEADS, head_dim))
        return (key_acc, value_acc), query_part

    (key_acc, value_acc), query_all = lax.scan(visit_block, initial, jnp.arange(NB, dtype=jnp.int32))
    return (query_all.reshape(TOKENS, width).astype(jnp.bfloat16),
            key_acc.reshape(TOKENS, width).astype(jnp.bfloat16),
            value_acc.reshape(TOKENS, width).astype(jnp.bfloat16))
```

```python
import functools

import jax
import jax.numpy as jnp
from jax import lax
from jax.experimental import pallas as pl
from jax.experimental.pallas import tpu as pltpu
from jax.sharding import PartitionSpec as P

BLK = 128
PACK = 2
FAR = 1.0e30

OWN, SIB, CROSS, RELAY, EDGE, TO, FROM = range(7)
SLOTS = 7
(G_SIB, G_CROSS, G_TO, G_FROM, G_RELAY1, G_RELAY2, G_EDGE,
 R_SIB, R_EDGE, R_FROM, R_RELAY1, R_RELAY2, R_CROSS, R_TO) = range(14)
KINDS = 14
NN = (((1,), (0,)), ((), ()))
NT = (((1,), (1,)), ((), ()))
TN = (((0,), (0,)), ((), ()))
MESH = pl.DeviceIdType.MESH


def kernel(devices, heads, q_hbm, k_hbm, v_hbm, g_hbm, stats_in, bias_ref, dq_hbm, dk_hbm, dv_hbm,
           buf, kv, stats, own_acc, cross_acc, relay_acc, to_acc, outgoing, returned, results,
           send_sem, recv_sem, stat_send, stat_recv, local_sem):
    group = lax.axis_index("groups")
    me = lax.axis_index("ctx")
    chunks = heads // PACK
    wide = PACK * 128
    core = me % 2
    chip_odd = (me // 2) % 2
    sign = 1 - 2 * chip_odd
    sib = me + 1 - 2 * core
    cross = me + 2 * sign
    relay = me - 2 * sign
    edge = me + 2 * core - 1
    to = me + 4 * sign
    frm = me - 4 * sign
    has_to = (to >= 0) & (to < devices)
    has_from = (frm >= 0) & (frm < devices)
    has_edge = (edge >= 0) & (edge < devices)
    sib_edge = sib - 2 * core + 1
    has_sib_edge = (sib_edge >= 0) & (sib_edge < devices)
    gives_cross = chip_odd == core
    factor = 128 ** (-0.5)

    def there(device):
        return (group, device)

    places = ((SIB, sib, None), (CROSS, cross, None), (RELAY, relay, has_from),
              (EDGE, edge, has_edge), (TO, to, has_to), (FROM, frm, has_from))
    mirror = {SIB: SIB, CROSS: CROSS, RELAY: RELAY, EDGE: EDGE, TO: FROM, FROM: TO}

    def guarded(condition, action):
        if condition is None:
            action()
        else:
            pl.when(condition)(action)

    loads = [pltpu.make_async_copy(source, target, local_sem.at[n]) for n, (source, target) in enumerate((
        (q_hbm, buf.at[0, pl.ds(0, BLK), :]), (g_hbm, buf.at[1, pl.ds(0, BLK), :]),
        (k_hbm, kv.at[0]), (v_hbm, kv.at[1])))]
    for load in loads:
        load.start()

    barrier = pltpu.get_barrier_semaphore()
    for _, device, present in places:
        guarded(present, lambda device=device: pl.semaphore_signal(
            barrier, inc=1, device_id=there(device), device_id_type=MESH))

    def blank(slot):
        buf[:, pl.ds(slot * BLK, BLK), :] = jnp.zeros((2, BLK, buf.shape[2]), buf.dtype)
        stats[slot] = jnp.zeros(stats.shape[1:], stats.dtype)

    for slot, _, present in places:
        if present is not None:
            pl.when(jnp.logical_not(present))(functools.partial(blank, slot))

    peers = 2 + sum(present.astype(jnp.int32) for _, _, present in places if present is not None)
    pl.semaphore_wait(barrier, peers)

    def stat_copy(slot, device):
        return pltpu.make_async_remote_copy(
            src_ref=stats_in, dst_ref=stats.at[mirror[slot]], send_sem=stat_send.at[slot],
            recv_sem=stat_recv.at[mirror[slot]], device_id=there(device), device_id_type=MESH)

    for slot, device, present in places:
        guarded(present, lambda slot=slot, device=device: stat_copy(slot, device).start())

    def columns(start, size):
        return pl.ds(pl.multiple_of(start, 128), size)

    def moved(kind, from_slot, to_slot, device, j, start, size):
        where = columns(start, size)
        return pltpu.make_async_remote_copy(
            src_ref=buf.at[:, pl.ds(from_slot * BLK, BLK), where],
            dst_ref=buf.at[:, pl.ds(to_slot * BLK, BLK), where],
            send_sem=send_sem.at[kind], recv_sem=recv_sem.at[kind, j],
            device_id=there(device), device_id_type=MESH)

    def handed(kind, slot, to_slot, device, j, start, size):
        where = columns(start, size)
        return pltpu.make_async_remote_copy(
            src_ref=outgoing.at[slot - 1, :, where],
            dst_ref=returned.at[to_slot - 1, :, where],
            send_sem=send_sem.at[kind], recv_sem=recv_sem.at[kind, j],
            device_id=there(device), device_id_type=MESH)

    half = wide // 2
    width = heads * 128
    copies = {
        G_SIB: lambda j, s, w: moved(G_SIB, OWN, SIB, sib, j, s, w),
        G_CROSS: lambda j, s, w: moved(G_CROSS, OWN, CROSS, cross, j, s, w),
        G_TO: lambda j, s, w: moved(G_TO, OWN, FROM, to, j, s, w),
        G_FROM: lambda j, s, w: moved(G_FROM, OWN, TO, frm, j, s, w),
        G_RELAY1: lambda j, s, w: moved(G_RELAY1, CROSS, RELAY, to, j, s, w),
        G_RELAY2: lambda j, s, w: moved(G_RELAY2, TO, RELAY, cross, j, s, w),
        R_SIB: lambda j, s, w: handed(R_SIB, SIB, SIB, sib, j, s, w),
        R_EDGE: lambda j, s, w: handed(R_EDGE, EDGE, EDGE, sib, j, s, w),
        R_FROM: lambda j, s, w: handed(R_FROM, FROM, TO, frm, j, s, w),
        R_RELAY1: lambda j, s, w: handed(R_RELAY1, RELAY, RELAY, frm, j, s, w),
        R_RELAY2: lambda j, s, w: handed(R_RELAY2, RELAY, RELAY, cross, j, s, w),
        R_CROSS: lambda j, s, w: handed(R_CROSS, CROSS, CROSS, cross, j, s, w),
        R_TO: lambda j, s, w: handed(R_TO, TO, FROM, to, j, s, w),
    }

    def begin(kind, j):
        offset = half if kind in (G_RELAY2, R_RELAY2) else 0
        size = half if kind in (G_RELAY1, G_RELAY2, R_RELAY1, R_RELAY2) else wide
        copies[kind](j, j * wide + offset, size).start()

    def begin_edge(slot, j):
        moved(G_EDGE, slot, EDGE, sib, j, j * wide, wide).start()

    def await_arrival(kind, j):
        if kind == G_EDGE:
            moved(G_EDGE, CROSS, EDGE, sib, j, j * wide, wide).wait_recv()
            return
        offset = half if kind in (G_RELAY2, R_RELAY2) else 0
        size = half if kind in (G_RELAY1, G_RELAY2, R_RELAY1, R_RELAY2) else wide
        copies[kind](j, j * wide + offset, size).wait_recv()

    def send_own(j):
        begin(G_CROSS, j)
        pl.when(has_to)(lambda: begin(G_TO, j))
        pl.when(has_from)(lambda: begin(G_FROM, j))
        begin(G_SIB, j)

    def relay_on(j):
        await_arrival(G_CROSS, j)

        @pl.when(has_to)
        def _():
            begin(G_RELAY1, j)
            await_arrival(G_FROM, j)
            begin(G_RELAY2, j)

        pl.when(gives_cross)(lambda: begin_edge(CROSS, j))

    def edge_on(j):
        @pl.when(has_from)
        def _():
            await_arrival(G_RELAY1, j)
            await_arrival(G_RELAY2, j)

        pl.when(jnp.logical_not(gives_cross) & has_from)(lambda: begin_edge(RELAY, j))

    def compute(j):
        await_arrival(G_SIB, j)
        pl.when(has_from)(lambda: await_arrival(G_TO, j))
        pl.when(has_edge)(lambda: await_arrival(G_EDGE, j))
        for n in range(PACK):
            h = j * PACK + n
            where = columns(h * 128, 128)
            keys, values = kv[0, :, where], kv[1, :, where]
            asked, cotangents = buf[0, :, where], buf[1, :, where]
            norms = jnp.concatenate([stats[s, pl.ds(h, 1), :] for s in range(SLOTS)], axis=1)
            deltas = jnp.concatenate([stats[s, pl.ds(heads + h, 1), :] for s in range(SLOTS)], axis=1)
            scores = lax.dot_general(keys, asked, NT, preferred_element_type=jnp.float32)
            probs = jnp.exp(scores * factor - norms)
            dprobs = lax.dot_general(values, cotangents, NT, preferred_element_type=jnp.float32)
            dscores = (probs * (dprobs - deltas)).astype(jnp.bfloat16)
            dv = lax.dot_general(probs.astype(jnp.bfloat16), cotangents, NN,
                                 preferred_element_type=jnp.float32)
            dk = lax.dot_general(dscores, asked, NN, preferred_element_type=jnp.float32)
            dq = lax.dot_general(dscores, keys, TN, preferred_element_type=jnp.float32) * factor
            results[1, :, where] = (dk * factor).astype(jnp.bfloat16)
            results[2, :, where] = dv.astype(jnp.bfloat16)

            def part(slot):
                return dq[slot * BLK:(slot + 1) * BLK]

            for slot in (SIB, EDGE, FROM):
                outgoing[slot - 1, :, where] = part(slot).astype(jnp.bfloat16)
            own_acc[:, where] = part(OWN)
            cross_acc[:, where] = part(CROSS)
            relay_acc[:, where] = part(RELAY)
            to_acc[:, where] = part(TO)
        pl.when(has_edge)(lambda: begin(R_EDGE, j))
        pl.when(has_from)(lambda: begin(R_FROM, j))
        begin(R_SIB, j)

    def back_relay(j):
        where = columns(j * wide, wide)

        @pl.when(has_sib_edge)
        def _():
            await_arrival(R_EDGE, j)

        @pl.when(gives_cross)
        def _():
            cross_acc[:, where] += returned[EDGE - 1, :, where].astype(jnp.float32)

        @pl.when(has_from)
        def _():
            @pl.when(jnp.logical_not(gives_cross))
            def _():
                relay_acc[:, where] += returned[EDGE - 1, :, where].astype(jnp.float32)

            outgoing[RELAY - 1, :, where] = relay_acc[:, where].astype(jnp.bfloat16)
            begin(R_RELAY1, j)
            begin(R_RELAY2, j)

    def back_direct(j):
        where = columns(j * wide, wide)
        first, second = columns(j * wide, half), columns(j * wide + half, half)

        @pl.when(has_to)
        def _():
            await_arrival(R_RELAY1, j)
            await_arrival(R_RELAY2, j)
            cross_acc[:, first] += returned[RELAY - 1, :, first].astype(jnp.float32)
            to_acc[:, second] += returned[RELAY - 1, :, second].astype(jnp.float32)
            outgoing[TO - 1, :, where] = to_acc[:, where].astype(jnp.bfloat16)
            begin(R_TO, j)

        outgoing[CROSS - 1, :, where] = cross_acc[:, where].astype(jnp.bfloat16)
        begin(R_CROSS, j)

    def finish(j):
        where = columns(j * wide, wide)
        await_arrival(R_SIB, j)
        await_arrival(R_CROSS, j)
        total = own_acc[:, where] + returned[SIB - 1, :, where].astype(jnp.float32)
        own_acc[:, where] = total + returned[CROSS - 1, :, where].astype(jnp.float32)

        @pl.when(has_to)
        def _():
            await_arrival(R_FROM, j)
            own_acc[:, where] += returned[TO - 1, :, where].astype(jnp.float32)

        @pl.when(has_from)
        def _():
            await_arrival(R_TO, j)
            own_acc[:, where] += returned[FROM - 1, :, where].astype(jnp.float32)

        results[0, :, where] = own_acc[:, where].astype(jnp.bfloat16)

    loads[0].wait()
    loads[1].wait()
    ahead = 2
    for j in range(ahead):
        send_own(j)
    loads[2].wait()
    loads[3].wait()
    stats[OWN] = stats_in[...]
    for slot, device, present in places:
        guarded(present, lambda slot=slot, device=device: stat_copy(mirror[slot], device).wait_recv())
    for slot in range(SLOTS):
        stats[slot, pl.ds(0, heads), :] += bias_ref[pl.ds(slot, 1), :]

    def step(t, carry):
        for lag, action in ((-ahead, send_own), (1, relay_on), (2, edge_on), (6, finish),
                            (5, back_direct), (4, back_relay), (3, compute)):
            j = t - lag
            pl.when((j >= max(0, -lag * (lag < 0))) & (j < chunks))(functools.partial(action, j))
        return carry

    lax.fori_loop(0, chunks + 6, step, 0)

    stores = [pltpu.make_async_copy(results.at[n], target, local_sem.at[n])
              for n, target in enumerate((dq_hbm, dk_hbm, dv_hbm))]
    for store in stores:
        store.start()
    for slot, device, present in places:
        guarded(present, lambda slot=slot, device=device: stat_copy(slot, device).wait_send())
    for kind, present in ((G_SIB, None), (G_CROSS, None), (G_TO, has_to), (G_FROM, has_from),
                          (G_RELAY1, has_to), (G_RELAY2, has_to), (R_SIB, None), (R_EDGE, has_edge),
                          (R_FROM, has_from), (R_RELAY1, has_from), (R_RELAY2, has_from),
                          (R_CROSS, None), (R_TO, has_to)):
        size = width // 2 if kind in (G_RELAY1, G_RELAY2, R_RELAY1, R_RELAY2) else width
        guarded(present, lambda kind=kind, size=size: copies[kind](0, 0, size).wait_send())
    pl.when(has_sib_edge)(lambda: moved(G_EDGE, CROSS, EDGE, sib, 0, 0, width).wait_send())
    for store in stores:
        store.wait()


def per_device(queries, key_states, value_states, out_grads, log_norms, row_deltas, kv_blocks):
    tok_rows, width = queries.shape
    heads = log_norms.shape[0]
    devices = lax.axis_size("ctx")
    me = lax.axis_index("ctx")
    sign = 1 - 2 * ((me // 2) % 2)
    core = me % 2
    asking = jnp.stack([me, me + 1 - 2 * core, me + 2 * sign, me - 2 * sign, me + 2 * core - 1,
                        me + 4 * sign, me - 4 * sign, me])
    inside = (asking >= 0) & (asking < devices)
    rows = kv_blocks[jnp.clip(asking, 0, devices - 1)]
    listed = jnp.any(rows == me, axis=1) & inside
    bias = jnp.broadcast_to(jnp.where(listed, 0.0, FAR).astype(jnp.float32)[:, None], (8, BLK))
    stats = jnp.concatenate([log_norms, row_deltas]).astype(jnp.float32)
    chunks = heads // PACK
    anywhere = pl.BlockSpec(memory_space=pl.ANY)
    in_vmem = pl.BlockSpec(memory_space=pltpu.VMEM)
    out = jax.ShapeDtypeStruct((tok_rows, width), jnp.bfloat16)
    return pl.pallas_call(
        functools.partial(kernel, devices, heads),
        out_shape=(out, out, out),
        in_specs=[anywhere] * 4 + [in_vmem] * 2,
        out_specs=(anywhere,) * 3,
        scratch_shapes=[
            pltpu.VMEM((2, SLOTS * BLK, width), jnp.bfloat16),
            pltpu.VMEM((2, BLK, width), jnp.bfloat16),
            pltpu.VMEM((SLOTS, 2 * heads, BLK), jnp.float32),
            pltpu.VMEM((BLK, width), jnp.float32),
            pltpu.VMEM((BLK, width), jnp.float32),
            pltpu.VMEM((BLK, width), jnp.float32),
            pltpu.VMEM((BLK, width), jnp.float32),
            pltpu.VMEM((SLOTS - 1, BLK, width), jnp.bfloat16),
            pltpu.VMEM((SLOTS - 1, BLK, width), jnp.bfloat16),
            pltpu.VMEM((3, BLK, width), jnp.bfloat16),
            pltpu.SemaphoreType.DMA((KINDS,)),
            pltpu.SemaphoreType.DMA((KINDS, chunks)),
            pltpu.SemaphoreType.DMA((SLOTS,)),
            pltpu.SemaphoreType.DMA((SLOTS,)),
            pltpu.SemaphoreType.DMA((4,)),
        ],
        compiler_params=pltpu.CompilerParams(
            collective_id=0, has_side_effects=True, vmem_limit_bytes=50 * 1024 * 1024),
        cost_estimate=pl.CostEstimate(
            flops=10 * heads * SLOTS * BLK * BLK * 128, bytes_accessed=14 * tok_rows * width,
            transcendentals=heads * SLOTS * BLK * BLK),
    )(queries, key_states, value_states, out_grads, stats, bias)


def solution(mesh):
    rows = P(("groups", "ctx"), None)
    lanes = P(None, ("groups", "ctx"))
    return jax.shard_map(
        per_device,
        mesh=mesh,
        in_specs=(rows, rows, rows, rows, lanes, lanes, P()),
        out_specs=(rows, rows, rows),
        check_vma=False,
    )
```

```python
import functools

import jax
import jax.numpy as jnp
from jax import lax
from jax.experimental import pallas as pl
from jax.experimental.pallas import tpu as pltpu
from jax.sharding import PartitionSpec as P

BLK = 128
PACK = 2
FAR = 1.0e30

OWN, SIB, CROSS, RELAY, EDGE, TO, FROM = range(7)
SLOTS = 7
(G_SIB, G_CROSS, G_TO, G_FROM, G_RELAY1, G_RELAY2, G_EDGE,
 R_SIB, R_EDGE, R_FROM, R_RELAY, R_CROSS, R_TO) = range(13)
KINDS = 13
AHEAD = 4
RELAY_LAG, EDGE_LAG, COMPUTE_LAG, BACK_RELAY_LAG, BACK_LAG, FINISH_LAG = 1, 3, 4, 5, 7, 9
DELTA_ROW = 24
NN = (((1,), (0,)), ((), ()))
NT = (((1,), (1,)), ((), ()))
TN = (((0,), (0,)), ((), ()))
MESH = pl.DeviceIdType.MESH


def kernel(devices, heads, q_hbm, k_hbm, v_hbm, g_hbm, norms_ref, deltas_ref, lists_ref,
           dq_hbm, dk_hbm, dv_hbm,
           buf, kv, stats, own_acc, cross_acc, relay_acc, outgoing, returned, results,
           send_sem, recv_sem, stat_send, stat_recv, local_sem):
    group = lax.axis_index("groups")
    me = lax.axis_index("ctx")
    chunks = heads // PACK
    wide = PACK * 128
    core = me % 2
    chip_odd = (me // 2) % 2
    sign = 1 - 2 * chip_odd
    sib = me + 1 - 2 * core
    cross = me + 2 * sign
    relay = me - 2 * sign
    edge = me + 2 * core - 1
    to = me + 4 * sign
    frm = me - 4 * sign
    has_to = (to >= 0) & (to < devices)
    has_from = (frm >= 0) & (frm < devices)
    has_edge = (edge >= 0) & (edge < devices)
    sib_edge = sib - 2 * core + 1
    has_sib_edge = (sib_edge >= 0) & (sib_edge < devices)
    gives_cross = chip_odd == core
    factor = 128 ** (-0.5)

    def there(device):
        return (group, device)

    places = ((SIB, sib, None), (CROSS, cross, None), (RELAY, relay, has_from),
              (EDGE, edge, has_edge), (TO, to, has_to), (FROM, frm, has_from))
    mirror = {SIB: SIB, CROSS: CROSS, RELAY: RELAY, EDGE: EDGE, TO: FROM, FROM: TO}

    def guarded(condition, action):
        if condition is None:
            action()
        else:
            pl.when(condition)(action)

    loads = [pltpu.make_async_copy(source, target, local_sem.at[n]) for n, (source, target) in enumerate((
        (q_hbm, buf.at[0, pl.ds(0, BLK), :]), (g_hbm, buf.at[1, pl.ds(0, BLK), :]),
        (k_hbm, kv.at[0]), (v_hbm, kv.at[1])))]
    for load in loads:
        load.start()

    barrier = pltpu.get_barrier_semaphore()
    stats[OWN] = jnp.zeros(stats.shape[1:], stats.dtype)
    stats[OWN, 0:heads, :] = norms_ref[...].astype(jnp.float32)
    stats[OWN, DELTA_ROW:DELTA_ROW + heads, :] = deltas_ref[...].astype(jnp.float32)
    for _, device, present in places:
        guarded(present, lambda device=device: pl.semaphore_signal(
            barrier, inc=1, device_id=there(device), device_id_type=MESH))

    def blank(slot):
        buf[:, pl.ds(slot * BLK, BLK), :] = jnp.zeros((2, BLK, buf.shape[2]), buf.dtype)
        stats[slot] = jnp.zeros(stats.shape[1:], stats.dtype)

    for slot, _, present in places:
        if present is not None:
            pl.when(jnp.logical_not(present))(functools.partial(blank, slot))

    peers = 2 + sum(present.astype(jnp.int32) for _, _, present in places if present is not None)
    pl.semaphore_wait(barrier, peers)

    def stat_copy(slot, device):
        return pltpu.make_async_remote_copy(
            src_ref=stats.at[OWN], dst_ref=stats.at[mirror[slot]], send_sem=stat_send.at[slot],
            recv_sem=stat_recv.at[mirror[slot]], device_id=there(device), device_id_type=MESH)


    def columns(start, size):
        return pl.ds(pl.multiple_of(start, 128), size)

    def moved(kind, from_slot, to_slot, device, j, start, size):
        where = columns(start, size)
        return pltpu.make_async_remote_copy(
            src_ref=buf.at[:, pl.ds(from_slot * BLK, BLK), where],
            dst_ref=buf.at[:, pl.ds(to_slot * BLK, BLK), where],
            send_sem=send_sem.at[kind], recv_sem=recv_sem.at[kind, j],
            device_id=there(device), device_id_type=MESH)

    def handed(kind, slot, to_slot, device, j, start, size):
        where = columns(start, size)
        return pltpu.make_async_remote_copy(
            src_ref=outgoing.at[slot - 1, :, where],
            dst_ref=returned.at[to_slot - 1, :, where],
            send_sem=send_sem.at[kind], recv_sem=recv_sem.at[kind, j],
            device_id=there(device), device_id_type=MESH)

    half = wide // 2
    width = heads * 128
    copies = {
        G_SIB: lambda j, s, w: moved(G_SIB, OWN, SIB, sib, j, s, w),
        G_CROSS: lambda j, s, w: moved(G_CROSS, OWN, CROSS, cross, j, s, w),
        G_TO: lambda j, s, w: moved(G_TO, OWN, FROM, to, j, s, w),
        G_FROM: lambda j, s, w: moved(G_FROM, OWN, TO, frm, j, s, w),
        G_RELAY1: lambda j, s, w: moved(G_RELAY1, CROSS, RELAY, to, j, s, w),
        G_RELAY2: lambda j, s, w: moved(G_RELAY2, TO, RELAY, cross, j, s, w),
        R_SIB: lambda j, s, w: handed(R_SIB, SIB, SIB, sib, j, s, w),
        R_EDGE: lambda j, s, w: handed(R_EDGE, EDGE, EDGE, sib, j, s, w),
        R_FROM: lambda j, s, w: handed(R_FROM, FROM, TO, frm, j, s, w),
        R_RELAY: lambda j, s, w: handed(R_RELAY, RELAY, RELAY, frm, j, s, w),
        R_CROSS: lambda j, s, w: handed(R_CROSS, CROSS, CROSS, cross, j, s, w),
        R_TO: lambda j, s, w: handed(R_TO, TO, FROM, to, j, s, w),
    }

    def begin(kind, j):
        offset = half if kind == G_RELAY2 else 0
        size = half if kind in (G_RELAY1, G_RELAY2) else wide
        copies[kind](j, j * wide + offset, size).start()

    def begin_edge(slot, j):
        moved(G_EDGE, slot, EDGE, sib, j, j * wide, wide).start()

    def await_arrival(kind, j):
        if kind == G_EDGE:
            moved(G_EDGE, CROSS, EDGE, sib, j, j * wide, wide).wait_recv()
            return
        offset = half if kind == G_RELAY2 else 0
        size = half if kind in (G_RELAY1, G_RELAY2) else wide
        copies[kind](j, j * wide + offset, size).wait_recv()

    def send_own(j):
        begin(G_CROSS, j)
        pl.when(has_to)(lambda: begin(G_TO, j))
        pl.when(has_from)(lambda: begin(G_FROM, j))
        begin(G_SIB, j)

    def relay_on(j):
        await_arrival(G_CROSS, j)

        @pl.when(has_to)
        def _():
            begin(G_RELAY1, j)
            await_arrival(G_FROM, j)
            begin(G_RELAY2, j)

        pl.when(gives_cross)(lambda: begin_edge(CROSS, j))

    def edge_on(j):
        @pl.when(has_from)
        def _():
            await_arrival(G_RELAY1, j)
            await_arrival(G_RELAY2, j)

        pl.when(jnp.logical_not(gives_cross) & has_from)(lambda: begin_edge(RELAY, j))

    def compute(j):
        await_arrival(G_SIB, j)
        pl.when(has_from)(lambda: await_arrival(G_TO, j))
        pl.when(has_edge)(lambda: await_arrival(G_EDGE, j))
        for n in range(PACK):
            h = j * PACK + n
            where = columns(h * 128, 128)
            keys, values = kv[0, :, where], kv[1, :, where]
            asked, cotangents = buf[0, :, where], buf[1, :, where]
            norms = jnp.concatenate([stats[s, pl.ds(h, 1), :] for s in range(SLOTS)], axis=1)
            deltas = jnp.concatenate([stats[s, pl.ds(DELTA_ROW + h, 1), :] for s in range(SLOTS)], axis=1)
            scores = lax.dot_general(keys, asked, NT, preferred_element_type=jnp.float32)
            probs = jnp.exp(scores * factor - norms)
            dprobs = lax.dot_general(values, cotangents, NT, preferred_element_type=jnp.float32)
            dscores = (probs * (dprobs - deltas)).astype(jnp.bfloat16)
            dv = lax.dot_general(probs.astype(jnp.bfloat16), cotangents, NN,
                                 preferred_element_type=jnp.float32)
            dk = lax.dot_general(dscores, asked, NN, preferred_element_type=jnp.float32)
            dq = lax.dot_general(dscores, keys, TN, preferred_element_type=jnp.float32) * factor
            results[1, :, where] = (dk * factor).astype(jnp.bfloat16)
            results[2, :, where] = dv.astype(jnp.bfloat16)

            def part(slot):
                return dq[slot * BLK:(slot + 1) * BLK]

            for slot in (SIB, EDGE, FROM, TO):
                outgoing[slot - 1, :, where] = part(slot).astype(jnp.bfloat16)
            own_acc[:, where] = part(OWN)
            cross_acc[:, where] = part(CROSS)
            relay_acc[:, where] = part(RELAY)
        pl.when(has_edge)(lambda: begin(R_EDGE, j))
        pl.when(has_from)(lambda: begin(R_FROM, j))
        pl.when(has_to)(lambda: begin(R_TO, j))
        begin(R_SIB, j)

    def back_relay(j):
        where = columns(j * wide, wide)

        @pl.when(has_sib_edge)
        def _():
            await_arrival(R_EDGE, j)

        @pl.when(gives_cross)
        def _():
            cross_acc[:, where] += returned[EDGE - 1, :, where].astype(jnp.float32)

        @pl.when(has_from)
        def _():
            @pl.when(jnp.logical_not(gives_cross))
            def _():
                relay_acc[:, where] += returned[EDGE - 1, :, where].astype(jnp.float32)

            outgoing[RELAY - 1, :, where] = relay_acc[:, where].astype(jnp.bfloat16)
            begin(R_RELAY, j)

    def back_direct(j):
        where = columns(j * wide, wide)

        @pl.when(has_to)
        def _():
            await_arrival(R_RELAY, j)
            cross_acc[:, where] += returned[RELAY - 1, :, where].astype(jnp.float32)

        outgoing[CROSS - 1, :, where] = cross_acc[:, where].astype(jnp.bfloat16)
        begin(R_CROSS, j)

    def finish(j):
        where = columns(j * wide, wide)
        await_arrival(R_SIB, j)
        await_arrival(R_CROSS, j)
        total = own_acc[:, where] + returned[SIB - 1, :, where].astype(jnp.float32)
        own_acc[:, where] = total + returned[CROSS - 1, :, where].astype(jnp.float32)

        @pl.when(has_to)
        def _():
            await_arrival(R_FROM, j)
            own_acc[:, where] += returned[TO - 1, :, where].astype(jnp.float32)

        @pl.when(has_from)
        def _():
            await_arrival(R_TO, j)
            own_acc[:, where] += returned[FROM - 1, :, where].astype(jnp.float32)

        results[0, :, where] = own_acc[:, where].astype(jnp.bfloat16)

    loads[0].wait()
    loads[1].wait()
    for j in range(AHEAD):
        send_own(j)
    for slot, device, present in places:
        guarded(present, lambda slot=slot, device=device: stat_copy(slot, device).start())
    loads[2].wait()
    loads[3].wait()
    for slot, device, present in places:
        guarded(present, lambda slot=slot, device=device: stat_copy(mirror[slot], device).wait_recv())
        guarded(present, lambda slot=slot, device=device: stat_copy(slot, device).wait_send())
    for slot, device, present in places:
        asking = device if present is None else jnp.where(present, device, 0)
        listed = lists_ref[0, asking] == me
        for n in range(1, lists_ref.shape[0]):
            listed = listed | (lists_ref[n, asking] == me)
        if present is not None:
            listed = listed & present
        stats[slot, 0:heads, :] += jnp.where(listed, 0.0, FAR)

    def step(t, carry):
        for lag, action in ((-AHEAD, send_own), (RELAY_LAG, relay_on), (EDGE_LAG, edge_on),
                            (FINISH_LAG, finish), (BACK_LAG, back_direct), (BACK_RELAY_LAG, back_relay),
                            (COMPUTE_LAG, compute)):
            j = t - lag
            pl.when((j >= max(0, -lag)) & (j < chunks))(functools.partial(action, j))
        return carry

    lax.fori_loop(0, chunks + FINISH_LAG, step, 0)

    stores = [pltpu.make_async_copy(results.at[n], target, local_sem.at[n])
              for n, target in enumerate((dq_hbm, dk_hbm, dv_hbm))]
    for store in stores:
        store.start()
    for kind, present in ((G_SIB, None), (G_CROSS, None), (G_TO, has_to), (G_FROM, has_from),
                          (G_RELAY1, has_to), (G_RELAY2, has_to), (R_SIB, None), (R_EDGE, has_edge),
                          (R_FROM, has_from), (R_RELAY, has_from),
                          (R_CROSS, None), (R_TO, has_to)):
        size = width // 2 if kind in (G_RELAY1, G_RELAY2) else width
        guarded(present, lambda kind=kind, size=size: copies[kind](0, 0, size).wait_send())
    pl.when(has_sib_edge)(lambda: moved(G_EDGE, CROSS, EDGE, sib, 0, 0, width).wait_send())
    for store in stores:
        store.wait()


def per_device(queries, key_states, value_states, out_grads, log_norms, row_deltas, kv_blocks):
    tok_rows, width = queries.shape
    heads = log_norms.shape[0]
    devices = lax.axis_size("ctx")
    chunks = heads // PACK
    anywhere = pl.BlockSpec(memory_space=pl.ANY)
    in_vmem = pl.BlockSpec(memory_space=pltpu.VMEM)
    out = jax.ShapeDtypeStruct((tok_rows, width), jnp.bfloat16)
    return pl.pallas_call(
        functools.partial(kernel, devices, heads),
        out_shape=(out, out, out),
        in_specs=[anywhere] * 4 + [in_vmem] * 2 + [pl.BlockSpec(memory_space=pltpu.SMEM)],
        out_specs=(anywhere,) * 3,
        scratch_shapes=[
            pltpu.VMEM((2, SLOTS * BLK, width), jnp.bfloat16),
            pltpu.VMEM((2, BLK, width), jnp.bfloat16),
            pltpu.VMEM((SLOTS, 2 * DELTA_ROW, BLK), jnp.float32),
            pltpu.VMEM((BLK, width), jnp.float32),
            pltpu.VMEM((BLK, width), jnp.float32),
            pltpu.VMEM((BLK, width), jnp.float32),
            pltpu.VMEM((SLOTS - 1, BLK, width), jnp.bfloat16),
            pltpu.VMEM((SLOTS - 1, BLK, width), jnp.bfloat16),
            pltpu.VMEM((3, BLK, width), jnp.bfloat16),
            pltpu.SemaphoreType.DMA((KINDS,)),
            pltpu.SemaphoreType.DMA((KINDS, chunks)),
            pltpu.SemaphoreType.DMA((SLOTS,)),
            pltpu.SemaphoreType.DMA((SLOTS,)),
            pltpu.SemaphoreType.DMA((4,)),
        ],
        compiler_params=pltpu.CompilerParams(
            collective_id=0, has_side_effects=True, vmem_limit_bytes=62 * 1024 * 1024),
        cost_estimate=pl.CostEstimate(
            flops=10 * heads * SLOTS * BLK * BLK * 128, bytes_accessed=14 * tok_rows * width,
            transcendentals=heads * SLOTS * BLK * BLK),
    )(queries, key_states, value_states, out_grads, log_norms, row_deltas, kv_blocks.T)


def solution(mesh):
    rows = P(("groups", "ctx"), None)
    lanes = P(None, ("groups", "ctx"))
    return jax.shard_map(
        per_device,
        mesh=mesh,
        in_specs=(rows, rows, rows, rows, lanes, lanes, P()),
        out_specs=(rows, rows, rows),
        check_vma=False,
    )
```

```python
import functools

import jax
import jax.numpy as jnp
from jax import lax
from jax.experimental import pallas as pl
from jax.experimental.pallas import tpu as pltpu
from jax.sharding import PartitionSpec as P

BLK = 128
PACK = 2
FAR = 1.0e30

OWN, SIB, CROSS, RELAY, EDGE, TO, FROM = range(7)
SLOTS = 7
(G_SIB, G_CROSS, G_TO, G_FROM, G_RELAY1, G_RELAY2, G_EDGE,
 R_SIB, R_EDGE, R_FROM, R_RELAY, R_CROSS, R_TO) = range(13)
KINDS = 13
AHEAD = 4
RELAY_LAG, EDGE_LAG, COMPUTE_LAG, BACK_RELAY_LAG, BACK_LAG, FINISH_LAG = 1, 3, 4, 5, 7, 9
PIECES = 4
DELTA_ROW = 24
NN = (((1,), (0,)), ((), ()))
NT = (((1,), (1,)), ((), ()))
TN = (((0,), (0,)), ((), ()))
MESH = pl.DeviceIdType.MESH


def kernel(devices, heads, q_hbm, k_hbm, v_hbm, g_hbm, norms_ref, deltas_ref, lists_ref,
           dq_hbm, dk_hbm, dv_hbm,
           buf, kv, stats, own_acc, cross_acc, relay_acc, outgoing, returned, results,
           send_sem, recv_sem, stat_send, stat_recv, local_sem, store_sem):
    group = lax.axis_index("groups")
    me = lax.axis_index("ctx")
    chunks = heads // PACK
    wide = PACK * 128
    core = me % 2
    chip_odd = (me // 2) % 2
    sign = 1 - 2 * chip_odd
    sib = me + 1 - 2 * core
    cross = me + 2 * sign
    relay = me - 2 * sign
    edge = me + 2 * core - 1
    to = me + 4 * sign
    frm = me - 4 * sign
    has_to = (to >= 0) & (to < devices)
    has_from = (frm >= 0) & (frm < devices)
    has_edge = (edge >= 0) & (edge < devices)
    sib_edge = sib - 2 * core + 1
    has_sib_edge = (sib_edge >= 0) & (sib_edge < devices)
    gives_cross = chip_odd == core
    factor = 128 ** (-0.5)

    def there(device):
        return (group, device)

    places = ((SIB, sib, None), (CROSS, cross, None), (RELAY, relay, has_from),
              (EDGE, edge, has_edge), (TO, to, has_to), (FROM, frm, has_from))
    mirror = {SIB: SIB, CROSS: CROSS, RELAY: RELAY, EDGE: EDGE, TO: FROM, FROM: TO}

    def guarded(condition, action):
        if condition is None:
            action()
        else:
            pl.when(condition)(action)

    loads = [pltpu.make_async_copy(source, target, local_sem.at[n]) for n, (source, target) in enumerate((
        (q_hbm, buf.at[0, pl.ds(0, BLK), :]), (g_hbm, buf.at[1, pl.ds(0, BLK), :]),
        (k_hbm, kv.at[0]), (v_hbm, kv.at[1])))]
    for load in loads:
        load.start()

    barrier = pltpu.get_barrier_semaphore()
    stats[OWN] = jnp.zeros(stats.shape[1:], stats.dtype)
    stats[OWN, 0:heads, :] = norms_ref[...].astype(jnp.float32)
    stats[OWN, DELTA_ROW:DELTA_ROW + heads, :] = deltas_ref[...].astype(jnp.float32)
    for _, device, present in places:
        guarded(present, lambda device=device: pl.semaphore_signal(
            barrier, inc=1, device_id=there(device), device_id_type=MESH))

    def blank(slot):
        buf[:, pl.ds(slot * BLK, BLK), :] = jnp.zeros((2, BLK, buf.shape[2]), buf.dtype)
        stats[slot] = jnp.zeros(stats.shape[1:], stats.dtype)

    for slot, _, present in places:
        if present is not None:
            pl.when(jnp.logical_not(present))(functools.partial(blank, slot))

    peers = 2 + sum(present.astype(jnp.int32) for _, _, present in places if present is not None)
    pl.semaphore_wait(barrier, peers)

    def stat_copy(slot, device):
        return pltpu.make_async_remote_copy(
            src_ref=stats.at[OWN], dst_ref=stats.at[mirror[slot]], send_sem=stat_send.at[slot],
            recv_sem=stat_recv.at[mirror[slot]], device_id=there(device), device_id_type=MESH)


    def columns(start, size):
        return pl.ds(pl.multiple_of(start, 128), size)

    def moved(kind, from_slot, to_slot, device, j, start, size):
        where = columns(start, size)
        return pltpu.make_async_remote_copy(
            src_ref=buf.at[:, pl.ds(from_slot * BLK, BLK), where],
            dst_ref=buf.at[:, pl.ds(to_slot * BLK, BLK), where],
            send_sem=send_sem.at[kind], recv_sem=recv_sem.at[kind, j],
            device_id=there(device), device_id_type=MESH)

    def handed(kind, slot, to_slot, device, j, start, size):
        where = columns(start, size)
        return pltpu.make_async_remote_copy(
            src_ref=outgoing.at[slot - 1, :, where],
            dst_ref=returned.at[to_slot - 1, :, where],
            send_sem=send_sem.at[kind], recv_sem=recv_sem.at[kind, j],
            device_id=there(device), device_id_type=MESH)

    half = wide // 2
    width = heads * 128
    copies = {
        G_SIB: lambda j, s, w: moved(G_SIB, OWN, SIB, sib, j, s, w),
        G_CROSS: lambda j, s, w: moved(G_CROSS, OWN, CROSS, cross, j, s, w),
        G_TO: lambda j, s, w: moved(G_TO, OWN, FROM, to, j, s, w),
        G_FROM: lambda j, s, w: moved(G_FROM, OWN, TO, frm, j, s, w),
        G_RELAY1: lambda j, s, w: moved(G_RELAY1, CROSS, RELAY, to, j, s, w),
        G_RELAY2: lambda j, s, w: moved(G_RELAY2, TO, RELAY, cross, j, s, w),
        R_SIB: lambda j, s, w: handed(R_SIB, SIB, SIB, sib, j, s, w),
        R_EDGE: lambda j, s, w: handed(R_EDGE, EDGE, EDGE, sib, j, s, w),
        R_FROM: lambda j, s, w: handed(R_FROM, FROM, TO, frm, j, s, w),
        R_RELAY: lambda j, s, w: handed(R_RELAY, RELAY, RELAY, frm, j, s, w),
        R_CROSS: lambda j, s, w: handed(R_CROSS, CROSS, CROSS, cross, j, s, w),
        R_TO: lambda j, s, w: handed(R_TO, TO, FROM, to, j, s, w),
    }

    def begin(kind, j):
        offset = half if kind == G_RELAY2 else 0
        size = half if kind in (G_RELAY1, G_RELAY2) else wide
        copies[kind](j, j * wide + offset, size).start()

    def begin_edge(slot, j):
        moved(G_EDGE, slot, EDGE, sib, j, j * wide, wide).start()

    def await_arrival(kind, j):
        if kind == G_EDGE:
            moved(G_EDGE, CROSS, EDGE, sib, j, j * wide, wide).wait_recv()
            return
        offset = half if kind == G_RELAY2 else 0
        size = half if kind in (G_RELAY1, G_RELAY2) else wide
        copies[kind](j, j * wide + offset, size).wait_recv()

    def store(n, target, start, size):
        where = columns(start, size)
        return pltpu.make_async_copy(results.at[n, :, where], target.at[:, where], store_sem.at[n])

    def send_own(j):
        begin(G_CROSS, j)
        pl.when(has_to)(lambda: begin(G_TO, j))
        pl.when(has_from)(lambda: begin(G_FROM, j))
        begin(G_SIB, j)

    def relay_on(j):
        await_arrival(G_CROSS, j)

        @pl.when(has_to)
        def _():
            begin(G_RELAY1, j)
            await_arrival(G_FROM, j)
            begin(G_RELAY2, j)

        pl.when(gives_cross)(lambda: begin_edge(CROSS, j))

    def edge_on(j):
        @pl.when(has_from)
        def _():
            await_arrival(G_RELAY1, j)
            await_arrival(G_RELAY2, j)

        pl.when(jnp.logical_not(gives_cross) & has_from)(lambda: begin_edge(RELAY, j))

    def compute(j):
        await_arrival(G_SIB, j)
        pl.when(has_from)(lambda: await_arrival(G_TO, j))
        pl.when(has_edge)(lambda: await_arrival(G_EDGE, j))
        for n in range(PACK):
            h = j * PACK + n
            where = columns(h * 128, 128)
            keys, values = kv[0, :, where], kv[1, :, where]
            asked, cotangents = buf[0, :, where], buf[1, :, where]
            norms = jnp.concatenate([stats[s, pl.ds(h, 1), :] for s in range(SLOTS)], axis=1)
            deltas = jnp.concatenate([stats[s, pl.ds(DELTA_ROW + h, 1), :] for s in range(SLOTS)], axis=1)
            scores = lax.dot_general(keys, asked, NT, preferred_element_type=jnp.float32)
            probs = jnp.exp(scores * factor - norms)
            dprobs = lax.dot_general(values, cotangents, NT, preferred_element_type=jnp.float32)
            dscores = (probs * (dprobs - deltas)).astype(jnp.bfloat16)
            dv = lax.dot_general(probs.astype(jnp.bfloat16), cotangents, NN,
                                 preferred_element_type=jnp.float32)
            dk = lax.dot_general(dscores, asked, NN, preferred_element_type=jnp.float32)
            dq = lax.dot_general(dscores, keys, TN, preferred_element_type=jnp.float32) * factor
            results[1, :, where] = (dk * factor).astype(jnp.bfloat16)
            results[2, :, where] = dv.astype(jnp.bfloat16)

            def part(slot):
                return dq[slot * BLK:(slot + 1) * BLK]

            for slot in (SIB, EDGE, FROM, TO):
                outgoing[slot - 1, :, where] = part(slot).astype(jnp.bfloat16)
            own_acc[:, where] = part(OWN)
            cross_acc[:, where] = part(CROSS)
            relay_acc[:, where] = part(RELAY)
        pl.when(has_edge)(lambda: begin(R_EDGE, j))
        pl.when(has_from)(lambda: begin(R_FROM, j))
        pl.when(has_to)(lambda: begin(R_TO, j))
        begin(R_SIB, j)

        for n, target in ((1, dk_hbm), (2, dv_hbm)):
            store(n, target, j * wide, wide).start()

    def back_relay(j):
        where = columns(j * wide, wide)

        @pl.when(has_sib_edge)
        def _():
            await_arrival(R_EDGE, j)

        @pl.when(gives_cross)
        def _():
            cross_acc[:, where] += returned[EDGE - 1, :, where].astype(jnp.float32)

        @pl.when(has_from)
        def _():
            @pl.when(jnp.logical_not(gives_cross))
            def _():
                relay_acc[:, where] += returned[EDGE - 1, :, where].astype(jnp.float32)

            outgoing[RELAY - 1, :, where] = relay_acc[:, where].astype(jnp.bfloat16)
            begin(R_RELAY, j)

    def back_direct(j):
        where = columns(j * wide, wide)

        @pl.when(has_to)
        def _():
            await_arrival(R_RELAY, j)
            cross_acc[:, where] += returned[RELAY - 1, :, where].astype(jnp.float32)

        outgoing[CROSS - 1, :, where] = cross_acc[:, where].astype(jnp.bfloat16)
        begin(R_CROSS, j)

    def finish(j):
        where = columns(j * wide, wide)
        await_arrival(R_SIB, j)
        await_arrival(R_CROSS, j)
        total = own_acc[:, where] + returned[SIB - 1, :, where].astype(jnp.float32)
        own_acc[:, where] = total + returned[CROSS - 1, :, where].astype(jnp.float32)

        @pl.when(has_to)
        def _():
            await_arrival(R_FROM, j)
            own_acc[:, where] += returned[TO - 1, :, where].astype(jnp.float32)

        @pl.when(has_from)
        def _():
            await_arrival(R_TO, j)
            own_acc[:, where] += returned[FROM - 1, :, where].astype(jnp.float32)

        results[0, :, where] = own_acc[:, where].astype(jnp.bfloat16)
        store(0, dq_hbm, j * wide, wide).start()

    loads[0].wait()
    loads[1].wait()
    for j in range(AHEAD):
        send_own(j)
    for slot, device, present in places:
        guarded(present, lambda slot=slot, device=device: stat_copy(slot, device).start())
    loads[2].wait()
    loads[3].wait()
    for slot, device, present in places:
        guarded(present, lambda slot=slot, device=device: stat_copy(mirror[slot], device).wait_recv())
        guarded(present, lambda slot=slot, device=device: stat_copy(slot, device).wait_send())
    for slot, device, present in places:
        asking = device if present is None else jnp.where(present, device, 0)
        listed = lists_ref[0, asking] == me
        for n in range(1, lists_ref.shape[0]):
            listed = listed | (lists_ref[n, asking] == me)
        if present is not None:
            listed = listed & present
        stats[slot, 0:heads, :] += jnp.where(listed, 0.0, FAR)

    def step(t, carry):
        for lag, action in ((RELAY_LAG, relay_on), (EDGE_LAG, edge_on), (BACK_LAG, back_direct), (BACK_RELAY_LAG, back_relay), (COMPUTE_LAG, compute),
                            (-AHEAD, send_own), (FINISH_LAG, finish)):
            j = t - lag
            pl.when((j >= max(0, -lag)) & (j < chunks))(functools.partial(action, j))
        return carry

    lax.fori_loop(0, chunks + FINISH_LAG, step, 0)

    for kind, present in ((G_SIB, None), (G_CROSS, None), (G_TO, has_to), (G_FROM, has_from),
                          (G_RELAY1, has_to), (G_RELAY2, has_to), (R_SIB, None), (R_EDGE, has_edge),
                          (R_FROM, has_from), (R_RELAY, has_from),
                          (R_CROSS, None), (R_TO, has_to)):
        size = width // 2 if kind in (G_RELAY1, G_RELAY2) else width
        guarded(present, lambda kind=kind, size=size: copies[kind](0, 0, size).wait_send())
    pl.when(has_sib_edge)(lambda: moved(G_EDGE, CROSS, EDGE, sib, 0, 0, width).wait_send())
    for n, target in enumerate((dq_hbm, dk_hbm, dv_hbm)):
        store(n, target, 0, width).wait()


def keep(dq_in, dk_in, dv_in, dq_out, dk_out, dv_out, held, in_sem, out_sem):
    size = held.shape[1] // PIECES
    arrays = ((dq_in, dq_out), (dk_in, dk_out), (dv_in, dv_out))
    pieces = [(n, p, pl.ds(p * size, size)) for p in range(PIECES) for n in range(3)]
    into = {(n, p): pltpu.make_async_copy(arrays[n][0].at[rows], held.at[n, rows], in_sem.at[n, p])
            for n, p, rows in pieces}
    out = {(n, p): pltpu.make_async_copy(held.at[n, rows], arrays[n][1].at[rows], out_sem.at[n, p])
           for n, p, rows in pieces}
    for n, p, _ in pieces:
        into[n, p].start()
    for n, p, _ in pieces:
        into[n, p].wait()
        out[n, p].start()
    for n, p, _ in pieces:
        out[n, p].wait()


def per_device(queries, key_states, value_states, out_grads, log_norms, row_deltas, kv_blocks):
    tok_rows, width = queries.shape
    heads = log_norms.shape[0]
    devices = lax.axis_size("ctx")
    chunks = heads // PACK
    anywhere = pl.BlockSpec(memory_space=pl.ANY)
    in_vmem = pl.BlockSpec(memory_space=pltpu.VMEM)
    out = jax.ShapeDtypeStruct((tok_rows, width), jnp.bfloat16)
    grads = pl.pallas_call(
        functools.partial(kernel, devices, heads),
        out_shape=(out, out, out),
        in_specs=[anywhere] * 4 + [in_vmem] * 2 + [pl.BlockSpec(memory_space=pltpu.SMEM)],
        out_specs=(anywhere,) * 3,
        scratch_shapes=[
            pltpu.VMEM((2, SLOTS * BLK, width), jnp.bfloat16),
            pltpu.VMEM((2, BLK, width), jnp.bfloat16),
            pltpu.VMEM((SLOTS, 2 * DELTA_ROW, BLK), jnp.float32),
            pltpu.VMEM((BLK, width), jnp.float32),
            pltpu.VMEM((BLK, width), jnp.float32),
            pltpu.VMEM((BLK, width), jnp.float32),
            pltpu.VMEM((SLOTS - 1, BLK, width), jnp.bfloat16),
            pltpu.VMEM((SLOTS - 1, BLK, width), jnp.bfloat16),
            pltpu.VMEM((3, BLK, width), jnp.bfloat16),
            pltpu.SemaphoreType.DMA((KINDS,)),
            pltpu.SemaphoreType.DMA((KINDS, chunks)),
            pltpu.SemaphoreType.DMA((SLOTS,)),
            pltpu.SemaphoreType.DMA((SLOTS,)),
            pltpu.SemaphoreType.DMA((4,)),
            pltpu.SemaphoreType.DMA((3,)),
        ],
        compiler_params=pltpu.CompilerParams(
            collective_id=0, has_side_effects=True, vmem_limit_bytes=62 * 1024 * 1024),
        cost_estimate=pl.CostEstimate(
            flops=10 * heads * SLOTS * BLK * BLK * 128, bytes_accessed=14 * tok_rows * width,
            transcendentals=heads * SLOTS * BLK * BLK),
    )(queries, key_states, value_states, out_grads, log_norms, row_deltas, kv_blocks.T)
    return pl.pallas_call(
        keep,
        out_shape=(out, out, out),
        in_specs=[anywhere] * 3,
        out_specs=(anywhere,) * 3,
        scratch_shapes=[
            pltpu.VMEM((3, BLK, width), jnp.bfloat16),
            pltpu.SemaphoreType.DMA((3, PIECES)),
            pltpu.SemaphoreType.DMA((3, PIECES)),
        ],
        compiler_params=pltpu.CompilerParams(vmem_limit_bytes=62 * 1024 * 1024),
        cost_estimate=pl.CostEstimate(flops=0, bytes_accessed=12 * tok_rows * width, transcendentals=0),
    )(*grads)


def solution(mesh):
    rows = P(("groups", "ctx"), None)
    lanes = P(None, ("groups", "ctx"))
    return jax.shard_map(
        per_device,
        mesh=mesh,
        in_specs=(rows, rows, rows, rows, lanes, lanes, P()),
        out_specs=(rows, rows, rows),
        check_vma=False,
    )
```
